32 devices in a mesh: gx: 8 (over z, x), gy: 4 (over y, core).
Axes of the slice: x: 2, y: 2, z: 4, core: 2. Of those that a mesh axis runs over, the one named last changes fastest.
Arguments:
- self_block: bfloat16 [16, 4, 2, 128, 128], P('gx', 'gy'), may hold values from -6 to 6
- coupling: bfloat16 [16, 4, 4, 2, 128, 128], P('gx', 'gy'), may hold values from -6 to 6
- skeleton: int32 [16, 4, 64], P('gx', 'gy'), may hold values from 0 to 127, as said below
- redundant: int32 [16, 4, 64], P('gx', 'gy'), may hold values from 0 to 127
- interp: bfloat16 [16, 4, 2, 64, 64], P('gx', 'gy'), may hold values from -0.5 to 0.5
- pivot: int32 [16, 4, 64], P('gx', 'gy'), may hold values from 0 to 63, each once within a row
- pivot_inverse: bfloat16 [16, 4, 2, 64, 64], P('gx', 'gy'), may hold values from -0.046875 to 0.046875
Outputs:
- factor: bfloat16 [16, 4, 5, 2, 64, 128], P('gx', 'gy')
- updated_self: bfloat16 [16, 4, 2, 128, 128], P('gx', 'gy')
- coarse: bfloat16 [8, 4, 2, 128, 128], P('gx', 'gy')
The draws below stay inside these ranges and needn't reach their ends.
Inputs may be any that keep to these rules, and one draw needn't show every extreme that they name: For each box, skeleton and redundant together list every point 0 to 127 exactly once.
All inputs are finite; a program needn't handle non-finite values.
Results may differ from the reference program's by a relative error of at most 0.0075.
Values may be sent and summed in bfloat16 or wider, within the bound.
A program may use at most 64 MiB of HBM per device.

```python
import jax
import jax.numpy as jnp
from jax import lax

P_SIZE = 128
S = 64
R = 64
HX = 1
NBX = 16
NBY = 4
N_GX = 8


def point_split(key):
    box_keys = jax.random.split(jax.random.fold_in(key, 11), NBX * NBY)
    orders = jax.vmap(lambda box_key: jax.random.permutation(box_key, P_SIZE))(box_keys)
    return orders.reshape(NBX, NBY, P_SIZE).astype(jnp.int32)


def draw_skeleton(key, part):
    return point_split(key)[:, :, :S]


def draw_redundant(key, part):
    return point_split(key)[:, :, S:]


def block_scale(rng, shape, cuts, least, top_value):
    factor_of, own = 1.0, jax.random.fold_in(rng, 6)
    for axis_at, parts in cuts:
        draws = jnp.exp(jax.random.uniform(jax.random.fold_in(own, axis_at), (parts,), jnp.float32, least / len(cuts), top_value / len(cuts)))
        factor_of = factor_of * jnp.repeat(draws, shape[axis_at] // parts).reshape([-1 if axis == axis_at else 1 for axis in range(len(shape))])
    return factor_of


def scatter_about(rng, shape, deviation, reach, cuts=(), dtype=jnp.bfloat16):
    loudness = block_scale(rng, shape, cuts, -0.22, 0.18) if cuts else 1.0
    entries = jax.random.normal(rng, shape, jnp.float32) * deviation * loudness
    return jnp.minimum(jnp.maximum(entries, -reach), reach).astype(dtype)


def setup_inputs(seed: int = 0) -> dict:
    seeds = jax.random.split(jax.random.key(seed), 8)
    self_block = scatter_about(seeds[0], (NBX, NBY, 2, P_SIZE, P_SIZE), 1.0, 6.0, ((0, 8), (1, 4)))
    coupling = scatter_about(seeds[1], (NBX, NBY, 4, 2, P_SIZE, P_SIZE), 1.0, 6.0, ((0, 8), (1, 4)))
    skeleton = draw_skeleton(jax.random.fold_in(seeds[7], 71), 0)
    redundant = draw_redundant(jax.random.fold_in(seeds[7], 71), 0)
    interp = scatter_about(seeds[4], (NBX, NBY, 2, S, R), (2 * S) ** -0.5, 0.5, ((0, 8), (1, 4)))
    pivot = jax.vmap(lambda own: jax.random.permutation(own, R))(jax.random.split(seeds[5], NBX * NBY)).reshape((NBX, NBY, R)).astype(jnp.int32)
    pivot_inverse = scatter_about(seeds[6], (NBX, NBY, 2, R, R), (0.5 / R), 0.046875, ((0, 8), (1, 4)))
    return {"self_block": self_block, "coupling": coupling, "skeleton": skeleton, "redundant": redundant, "interp": interp, "pivot": pivot, "pivot_inverse": pivot_inverse}


def complex_product(pattern, left_op, right_op):
    def single(first_op, second_op):
        return jnp.einsum(pattern, first_op.astype(jnp.float32), second_op.astype(jnp.float32))
    real_part = single(left_op[:, 0], right_op[:, 0]) - single(left_op[:, 1], right_op[:, 1])
    imag_part = single(left_op[:, 0], right_op[:, 1]) + single(left_op[:, 1], right_op[:, 0])
    return jnp.stack([real_part, imag_part], 1)


def rows_of(block_in, indices):
    shape = (block_in.shape[0], 2, indices.shape[1], block_in.shape[3])
    return jnp.take_along_axis(block_in, jnp.broadcast_to(indices[:, None, :, None], shape), axis=2)


def cols_of(block_in, indices):
    shape = (block_in.shape[0], 2, block_in.shape[2], indices.shape[1])
    return jnp.take_along_axis(block_in, jnp.broadcast_to(indices[:, None, None, :], shape), axis=3)


def eliminate(box_data, block_in):
    skel_index, red_index, interp_blk, pivot_order, inverse = box_data
    reduced = rows_of(block_in, red_index).astype(jnp.float32) - complex_product("bsr,bsn->brn", interp_blk, rows_of(block_in, skel_index))
    reduced = reduced.astype(jnp.bfloat16)
    return complex_product("bij,bjn->bin", inverse, rows_of(reduced, pivot_order)).astype(jnp.bfloat16)


def couple_in(box_data, block_in):
    skel_index = box_data[0]
    red_index = box_data[1]
    interp_blk = box_data[2]
    result = cols_of(block_in, red_index).astype(jnp.float32) - complex_product("bms,bsr->bmr", cols_of(block_in, skel_index), interp_blk)
    return result.astype(jnp.bfloat16)


def reference(self_block, coupling, skeleton, redundant, interp, pivot, pivot_inverse):
    def pick(array_in, position):
        return lax.dynamic_index_in_dim(array_in, position, 0, keepdims=False)

    def box_data(position):
        return tuple(pick(array_in, position) for array_in in (skeleton, redundant, interp, pivot, pivot_inverse))

    even_rows = (jnp.arange(NBY) % 2 == 0)[:, None, None, None]

    def column(position):
        before = ((position + NBX - 1) % NBX).astype(jnp.int32)
        after = ((position + 1) % NBX).astype(jnp.int32)
        own_block = pick(self_block, position)
        here_pairs = pick(coupling, position)
        left_pairs = pick(coupling, before)
        data_here = box_data(position)
        outgoing = [own_block, left_pairs[:, 1], here_pairs[:, 0], jnp.roll(here_pairs[:, 3], 1, 0), here_pairs[:, 2]]
        factors = [eliminate(data_here, block_in) for block_in in outgoing]
        below_update = complex_product("bmr,brn->bmn", couple_in(data_here, jnp.roll(here_pairs[:, 2], 1, 0)), factors[3])
        above_update = complex_product("bmr,brn->bmn", couple_in(data_here, here_pairs[:, 3]), factors[4])
        data_before = box_data(before)
        from_left = complex_product("bmr,brn->bmn", couple_in(data_before, left_pairs[:, 1]), eliminate(data_before, left_pairs[:, 0]))
        data_after = box_data(after)
        from_right = complex_product("bmr,brn->bmn", couple_in(data_after, here_pairs[:, 0]), eliminate(data_after, here_pairs[:, 1]))
        total_blk = own_block.astype(jnp.float32) - (from_left + from_right + jnp.roll(above_update, 1, 0) + jnp.roll(below_update, -1, 0))
        skel_index = data_here[0]
        skel_self = rows_of(own_block, skel_index)
        edge_zero = cols_of(skel_self, data_here[1]).astype(jnp.float32) - complex_product("bsu,bur->bsr", cols_of(skel_self, skel_index), data_here[2])
        edge_zero = edge_zero.astype(jnp.bfloat16)
        skel_rows = (rows_of(total_blk, skel_index) - complex_product("bsr,brn->bsn", edge_zero, factors[0])).astype(jnp.bfloat16)
        cross_up = rows_of(outgoing[4], skel_index).astype(jnp.float32) - complex_product("bsr,brn->bsn", edge_zero, factors[4])
        cross_down = rows_of(outgoing[3], skel_index).astype(jnp.float32) - complex_product("bsr,brn->bsn", edge_zero, factors[3])
        cross_rows = jnp.where(even_rows, cross_up, cross_down).astype(jnp.bfloat16)
        lower_skel = skel_index[0::2]
        upper_skel = skel_index[1::2]
        top_rows = jnp.concatenate([cols_of(skel_rows[0::2], lower_skel), cols_of(cross_rows[0::2], upper_skel)], -1)
        bottom_rows = jnp.concatenate([cols_of(cross_rows[1::2], lower_skel), cols_of(skel_rows[1::2], upper_skel)], -1)
        return jnp.stack(factors, 1), total_blk.astype(jnp.bfloat16), jnp.concatenate([top_rows, bottom_rows], -2)

    factor, updated, coarse = lax.map(column, jnp.arange(NBX).astype(jnp.int32))
    coarse = coarse.reshape(N_GX, 2, HX, NBY // 2, 2, 2 * S, 2 * S)
    coarse = coarse.transpose(0, 2, 3, 1, 4, 5, 6).reshape(N_GX * HX, NBY, 2, 2 * S, 2 * S)
    return factor, updated, coarse
```

```python
import jax
import jax.numpy as jnp
from jax import lax
from jax.sharding import PartitionSpec as P


def from_behind(value, axis, steps):
    count = lax.axis_size(axis)
    pairs = [(source, (source + steps) % count) for source in range(count)]
    return lax.ppermute(value, axis, pairs)


def padded(cells, sides, width):
    for axis, dim in sides:
        count = lax.axis_size(axis)
        head = lax.slice_in_dim(cells, 0, width, axis=dim)
        tail = lax.slice_in_dim(cells, cells.shape[dim] - width, cells.shape[dim], axis=dim)
        cells = jnp.concatenate(
            [
                lax.ppermute(tail, axis, [(i, (i + 1) % count) for i in range(count)]),
                cells,
                lax.ppermute(head, axis, [((i + 1) % count, i) for i in range(count)]),
            ],
            axis=dim,
        )
    return cells


def swapped(value, axis, distance):
    mask = 2**distance
    pairs = [(source, source ^ mask) for source in range(lax.axis_size(axis))]
    return lax.ppermute(value, axis, pairs)


def complex_product(first, second, output, left_op, right_op):
    mixed = jnp.stack(
        [
            jnp.stack([right_op[:, 0], right_op[:, 1]], 1),
            jnp.stack([-right_op[:, 1], right_op[:, 0]], 1),
        ],
        1,
    )
    form = (
        first[0]
        + "c"
        + first[1:]
        + ","
        + second[0]
        + "ce"
        + second[1:]
        + "->"
        + output[0]
        + "e"
        + output[1:]
    )
    return jnp.einsum(form, left_op, mixed, preferred_element_type=jnp.float32)


def select_rows(selector, block_in):
    return jnp.einsum(
        "bsp,bcpn->bcsn", selector, block_in, preferred_element_type=jnp.float32
    ).astype(jnp.bfloat16)


def outgoing_factor(qt_mat, pivot_inv, block_in):
    reduced = complex_product("brp", "bpn", "brn", qt_mat, block_in).astype(jnp.bfloat16)
    return complex_product("bij", "bjn", "bin", pivot_inv, reduced).astype(jnp.bfloat16)


def incoming_factor(qt_mat, block_in):
    return complex_product("brp", "bmp", "brm", qt_mat, block_in).astype(jnp.bfloat16)


def rank_update(left_t, right_op):
    return complex_product("brm", "brn", "bmn", left_t, right_op)


def prepare(skel_index, red_index, interp_blk, pivot_order, inverse, points):
    point_ids = lax.iota(jnp.int32, points)
    pick_skel = (skel_index[:, :, None] == point_ids).astype(jnp.bfloat16)
    pick_red = (red_index[:, :, None] == point_ids).astype(jnp.bfloat16)
    spread = jnp.einsum("bcsr,bsp->bcrp", interp_blk, pick_skel, preferred_element_type=jnp.float32)
    qt_mat = jnp.stack([pick_red.astype(jnp.float32) - spread[:, 0], -spread[:, 1]], 1).astype(
        jnp.bfloat16
    )
    pivot_pick = (pivot_order[:, :, None] == lax.iota(jnp.int32, pivot_order.shape[-1])).astype(
        jnp.bfloat16
    )
    pivot_inv = jnp.einsum(
        "bcai,bij->bcaj", inverse, pivot_pick, preferred_element_type=jnp.float32
    ).astype(jnp.bfloat16)
    return (pick_skel, qt_mat, pivot_inv)


def local(self_block, coupling, skeleton, redundant, interp, pivot, pivot_inverse):
    own_block = self_block[:, 0]
    couple_pairs = coupling[:, 0]
    skel_index = skeleton[:, 0]
    red_index = redundant[:, 0]
    interp_blk = interp[:, 0]
    pivot_order = pivot[:, 0]
    inverse = pivot_inverse[:, 0]
    box_count = own_block.shape[0]
    half_count = box_count // 2
    points = own_block.shape[-1]
    skel_size = skel_index.shape[-1]
    pick_skel, qt_mat, pivot_inv = prepare(
        skel_index, red_index, interp_blk, pivot_order, inverse, points
    )
    edge_pairs = from_behind(couple_pairs[box_count - 1 :, 0:2], "gx", 1)
    left_pairs = jnp.concatenate([edge_pairs, couple_pairs[:-1, 0:2]], 0)
    own_factor = outgoing_factor(qt_mat, pivot_inv, own_block)
    left_factor = outgoing_factor(qt_mat, pivot_inv, left_pairs[:, 1])
    right_factor = outgoing_factor(qt_mat, pivot_inv, couple_pairs[:, 0])
    up_factor = outgoing_factor(qt_mat, pivot_inv, couple_pairs[:, 2])
    left_term = incoming_factor(qt_mat, left_pairs[:, 0])
    right_term = incoming_factor(qt_mat, couple_pairs[:, 1])
    up_term = incoming_factor(qt_mat, couple_pairs[:, 3])
    left_update = rank_update(left_term, left_factor)
    right_update = rank_update(right_term, right_factor)
    edge_send = jnp.stack([left_update[0], right_update[box_count - 1]], 0)
    edge_recv = padded(edge_send.astype(jnp.bfloat16), (("gx", 0),), 1).astype(edge_send.dtype)
    from_left = jnp.concatenate([edge_recv[0:1], right_update[:-1]], 0)
    from_right = jnp.concatenate([left_update[1:], edge_recv[3:4]], 0)
    lower_pairs = from_behind(couple_pairs[:, 2:4], "gy", 1)
    down_factor = outgoing_factor(qt_mat, pivot_inv, lower_pairs[:, 1])
    down_term = incoming_factor(qt_mat, lower_pairs[:, 0])
    down_rows = select_rows(pick_skel, lower_pairs[:, 1])
    row_send = jnp.stack([rank_update(down_term, down_factor), rank_update(up_term, up_factor)], 1)
    row_recv = padded(row_send.astype(jnp.bfloat16), (("gy", 1),), 1).astype(row_send.dtype)
    from_below = row_recv[:, 0]
    from_above = row_recv[:, 3]
    total_blk = own_block.astype(jnp.float32) - (from_left + from_right + from_below + from_above)
    updated = total_blk.astype(jnp.bfloat16)
    rest = (total_blk - updated.astype(jnp.float32)).astype(jnp.bfloat16)
    total_rows = jnp.einsum(
        "bsp,bcpn->bcsn", pick_skel, updated, preferred_element_type=jnp.float32
    ) + jnp.einsum("bsp,bcpn->bcsn", pick_skel, rest, preferred_element_type=jnp.float32)
    skel_self = select_rows(pick_skel, own_block)
    edge_zero = complex_product("bsp", "brp", "bsr", skel_self, qt_mat).astype(jnp.bfloat16)
    skel_rows = (total_rows - complex_product("bsr", "brn", "bsn", edge_zero, own_factor)).astype(
        jnp.bfloat16
    )
    lower_side = lax.axis_index("gy") % 2 == 0
    up_rows = select_rows(pick_skel, couple_pairs[:, 2])
    toward_rows = jnp.where(lower_side, up_rows, down_rows)
    toward_factor = jnp.where(lower_side, up_factor, down_factor)
    cross_rows = (
        toward_rows.astype(jnp.float32)
        - complex_product("bsr", "brn", "bsn", edge_zero, toward_factor)
    ).astype(jnp.bfloat16)
    skel_block = jnp.einsum(
        "bcsp,btp->bcst", skel_rows, pick_skel, preferred_element_type=jnp.float32
    ).astype(jnp.bfloat16)
    skel_packed = jnp.concatenate([skel_block[:, 0], skel_block[:, 1]], -1)
    send_pack = jnp.stack([cross_rows[:, 0], cross_rows[:, 1], skel_packed, pick_skel], 1)
    send_half = jnp.where(lower_side, send_pack[half_count:], send_pack[:half_count])
    partner_pack = swapped(send_half, "gy", 0)
    kept_cross = jnp.where(lower_side, cross_rows[:half_count], cross_rows[half_count:])
    kept_skel = jnp.where(lower_side, skel_block[:half_count], skel_block[half_count:])
    kept_pick = jnp.where(lower_side, pick_skel[:half_count], pick_skel[half_count:])
    partner_skel = jnp.stack(
        [partner_pack[:, 2, :, :skel_size], partner_pack[:, 2, :, skel_size:]], 1
    )
    own_coupling = jnp.einsum(
        "bcsp,btp->bcst", kept_cross, partner_pack[:, 3], preferred_element_type=jnp.float32
    ).astype(jnp.bfloat16)
    partner_coupling = jnp.einsum(
        "bcsp,btp->bcst", partner_pack[:, 0:2], kept_pick, preferred_element_type=jnp.float32
    ).astype(jnp.bfloat16)
    lower_skel = jnp.where(lower_side, kept_skel, partner_skel)
    upper_skel = jnp.where(lower_side, partner_skel, kept_skel)
    upper_right = jnp.where(lower_side, own_coupling, partner_coupling)
    lower_left = jnp.where(lower_side, partner_coupling, own_coupling)
    top_rows = jnp.concatenate([lower_skel, upper_right], -1)
    bottom_rows = jnp.concatenate([lower_left, upper_skel], -1)
    coarse = jnp.concatenate([top_rows, bottom_rows], -2)[:, None]
    factor = jnp.stack([own_factor, left_factor, right_factor, down_factor, up_factor], 1)[:, None]
    return (factor, updated[:, None], coarse)


def solution(mesh):
    placed = (
        P("gx", "gy", None, None, None),
        P("gx", "gy", None, None, None, None),
        P("gx", "gy", None),
        P("gx", "gy", None),
        P("gx", "gy", None, None, None),
        P("gx", "gy", None),
        P("gx", "gy", None, None, None),
    )
    return jax.shard_map(
        local,
        mesh=mesh,
        in_specs=placed,
        out_specs=(
            P("gx", "gy", None, None, None, None),
            P("gx", "gy", None, None, None),
            P("gx", "gy", None, None, None),
        ),
        check_vma=False,
    )
```

```python
import jax
import jax.numpy as jnp
from jax import lax
from jax.experimental import pallas as pl
from jax.experimental.pallas import tpu as pltpu
from jax.sharding import PartitionSpec as P

MESH = pl.DeviceIdType.MESH
BF16, F32 = jnp.bfloat16, jnp.float32


def dot(left_op, right_op):
    return jnp.dot(left_op, right_op, preferred_element_type=F32)


def dot_nt(left_op, right_op):
    return lax.dot_general(left_op, right_op, (((1,), (1,)), ((), ())), preferred_element_type=F32)


def cat(axis, *parts):
    return jnp.concatenate(parts, axis)


def beside(ref, *index):
    return cat(1, ref[(*index, 0)], ref[(*index, 1)])


def above(ref, *index):
    return cat(0, ref[(*index, 0)], ref[(*index, 1)])


def folded(wide):
    half = wide.shape[1] // 2
    return cat(0, wide[:, :half], wide[:, half:])


def paired(tall):
    half = tall.shape[0] // 2
    return cat(1, tall[:half], tall[half:])


def make_params(par, pick, skel, red, interp, pivot, inverse, j):
    points, size = pick.shape[2], skel.shape[2]
    ids = lax.broadcasted_iota(jnp.int32, (points, size), 0)
    skel_t = jnp.where(ids == skel[j], 1.0, 0.0)
    red_t = jnp.where(ids == red[j], 1.0, 0.0)
    order = jnp.where(ids[:size] == pivot[j], 1.0, 0.0).astype(BF16)
    spread = dot(skel_t.astype(BF16), beside(interp, j))
    q_t = cat(1, red_t, jnp.zeros_like(red_t)) - spread
    par[j, 0 : 2 * size, :] = q_t.T.astype(BF16)
    turned = dot_nt(above(inverse, j), order).astype(BF16)
    par[j, 2 * size : 3 * size, :] = paired(turned)
    pick[j] = cat(1, skel_t, red_t).T[:size].astype(BF16)


def read_params(block):
    size = block.shape[0] // 3
    q_re, q_im, inv = block[:size], block[size : 2 * size], block[2 * size :]
    real_row, imag_row = cat(1, q_re, -q_im), cat(1, q_im, q_re)
    q_mix = cat(0, real_row, imag_row)
    e_mix = cat(0, real_row, -imag_row, imag_row, real_row)
    inv_re, inv_im = inv[:, :size], inv[:, size:]
    inv_mix = cat(0, cat(1, inv_re, -inv_im), cat(1, inv_im, inv_re))
    return q_mix, e_mix, inv_mix


def factors(params, right_op):
    q_mix, _, inv_mix = params
    return dot(inv_mix, dot(q_mix, right_op).astype(BF16)).astype(BF16)


def kernel(
    self_hbm, coup_hbm, skel_hbm, red_hbm, interp_hbm, pivot_hbm, inverse_hbm,
    factor_out, updated_out, coarse_out,
    own, coup, skel, red, interp, pivot, inverse,
    pick, par, par_x, par_y, extra, extra_y, fac, acc, w_send_x, w_send_y, w_x, w_y,
    self_term, keep_k, g_own, g_other, updated, coarse,
    in_sem, send_sem, recv_sem, out_sem,
):
    n, points = own.shape[0], own.shape[2]
    half, size = n // 2, skel.shape[2]
    gx, gy = lax.axis_index("gx"), lax.axis_index("gy")
    nx, ny = lax.axis_size("gx"), lax.axis_size("gy")
    x_next, x_back = {"gx": lax.rem(gx + 1, nx)}, {"gx": lax.rem(gx + nx - 1, nx)}
    y_next, y_back = {"gy": lax.rem(gy + 1, ny)}, {"gy": lax.rem(gy + ny - 1, ny)}
    odd = lax.rem(gy, 2)
    partner = {"gy": gy + 1 - 2 * odd}

    barrier = pltpu.get_barrier_semaphore()
    for device in (x_next, x_back, y_next, y_back):
        pl.semaphore_signal(barrier, inc=1, device_id=device, device_id_type=MESH)

    def load(source, target, at):
        copy = pltpu.make_async_copy(source, target, in_sem.at[at])
        copy.start()
        return copy

    small = [
        load(skel_hbm, skel, 0),
        load(red_hbm, red, 1),
        load(interp_hbm.at[:, 0], interp, 2),
        load(pivot_hbm, pivot, 3),
        load(inverse_hbm.at[:, 0], inverse, 4),
    ]
    large = []
    for j in range(n):
        large.append(
            (
                load(coup_hbm.at[j, 0], coup.at[j], 5 + 2 * j),
                load(self_hbm.at[j, 0], own.at[j], 6 + 2 * j),
            )
        )

    def remote(source, target, at, device):
        return pltpu.make_async_remote_copy(
            src_ref=source, dst_ref=target, send_sem=send_sem.at[at],
            recv_sem=recv_sem.at[at], device_id=device, device_id_type=MESH,
        )

    outs = []

    def store(source, target):
        copy = pltpu.make_async_copy(source, target, out_sem.at[len(outs)])
        copy.start()
        outs.append(copy)

    send_par_x = remote(par.at[0], par_x, 0, x_back)
    send_par_y = remote(par, par_y, 1, y_back)
    send_extra = remote(extra, extra_y, 2, y_back)
    send_w_x = remote(w_send_x, w_x, 3, x_next)
    send_k = remote(keep_k.at[pl.ds(half, half)], keep_k.at[pl.ds(0, half)], 4, partner)
    send_g = remote(g_own.at[pl.ds((1 - odd) * half, half)], g_other, 5, partner)
    send_fac_x = remote(fac.at[n - 1, 1], factor_out.at[0, 0, 1], 6, x_next)
    send_w_y = [remote(w_send_y.at[j], w_y.at[j], 7 + 2 * j, y_next) for j in range(n)]
    send_fac_y = [
        remote(fac.at[j, 3], factor_out.at[j, 0, 3], 8 + 2 * j, y_next) for j in range(n)
    ]

    def put_factor(j, k, value):
        fac[j, k] = value.reshape(2, size, points)

    for copy in small:
        copy.wait()
    for j in range(n):
        make_params(par, pick, skel, red, interp, pivot, inverse, j)
    pl.semaphore_wait(barrier, 4)
    send_par_y.start()
    send_par_x.start()

    for j in range(n):
        for copy in large[j]:
            copy.wait()
    params = [read_params(par[j]) for j in range(n)]
    w_right = []
    for j in range(n):
        right_ops = cat(1, above(coup, j, 2), above(coup, j, 0), above(own, j))
        made = factors(params[j], right_ops)
        f_up, f_right, f_own = (made[:, k * points : (k + 1) * points] for k in range(3))
        put_factor(j, 4, f_up)
        put_factor(j, 2, f_right)
        put_factor(j, 0, f_own)
        own_rows = dot(pick[j], beside(own, j)).astype(BF16)
        left_ops = cat(0, beside(coup, j, 3), beside(coup, j, 1), own_rows)
        ends = dot_nt(left_ops, params[j][1]).astype(BF16)
        w_send_y[j] = dot(folded(ends[:points]), f_up).astype(BF16)
        send_w_y[j].start()
        w_right.append(dot(folded(ends[points : 2 * points]), f_right))
        if j == n - 1:
            w_send_x[...] = w_right[j].astype(BF16)
            send_w_x.start()
        e_mix = folded(ends[2 * points :])
        self_term[j] = dot(e_mix, cat(1, f_own, f_up))
        extra[j, :size, :] = cat(1, e_mix[:size, :size], e_mix[size:, :size])
        extra[j, size:, :] = pick[j]
        acc[j] = above(own, j).astype(F32)
        if j > 0:
            acc[j] = acc[j] - w_right[j - 1]

    @pl.when(odd == 1)
    def _():
        send_extra.start()

    for j in range(n):
        for k in (0, 2, 4):
            store(fac.at[j, k], factor_out.at[j, 0, k])

    def from_next(next_params, j, k):
        made = factors(next_params, above(coup, j, k))
        put_factor(j, k, made)
        ends = dot_nt(beside(coup, j, k - 1), next_params[1]).astype(BF16)
        return made, dot(folded(ends), made)

    for j in range(n - 1):
        acc[j] = acc[j] - from_next(params[j + 1], j, 1)[1]
        store(fac.at[j, 1], factor_out.at[j + 1, 0, 1])
    send_par_y.wait_recv()
    for j in range(n):
        acc[j] = acc[j] - from_next(read_params(par_y[j]), j, 3)[1]
        send_fac_y[j].start()
    send_par_x.wait_recv()
    acc[n - 1] = acc[n - 1] - from_next(read_params(par_x[...]), n - 1, 1)[1]
    send_fac_x.start()

    @pl.when(odd == 0)
    def _():
        send_extra.wait_recv()
        for j in reversed(range(n)):
            lower_pick, upper_pick = pick[j], extra_y[j, size:, :]
            rows = folded(dot(lower_pick, beside(coup, j, 2))) - self_term[j, :, points:]
            keep_k[j, 0] = paired(dot_nt(rows.astype(BF16), upper_pick).astype(BF16))
            end = extra_y[j, :size, :]
            e_re, e_im = end[:, :size], end[:, size:]
            e_mix = cat(0, cat(1, e_re, -e_im), cat(1, e_im, e_re))
            upper_factor = above(fac, j, 3)
            rows = folded(dot(upper_pick, beside(coup, j, 3))) - dot(e_mix, upper_factor)
            keep_k[j, 1] = paired(dot_nt(rows.astype(BF16), lower_pick).astype(BF16))
        send_k.start()

    send_w_x.wait_recv()
    for j in range(n):
        send_w_y[j].wait_recv()
    for j in range(n):
        total = acc[j] - w_y[j].astype(F32)
        if j == 0:
            total = total - w_x[...].astype(F32)
        rounded = total.astype(BF16)
        rest = (total - rounded.astype(F32)).astype(BF16)
        updated[j] = rounded.reshape(2, points, points)
        rows = dot(pick[j], cat(1, paired(rounded), paired(rest)))
        rows = rows[:, : 2 * points] + rows[:, 2 * points :]
        rows = (folded(rows) - self_term[j, :, :points]).astype(BF16)
        g_own[j] = paired(dot_nt(rows, pick[j]).astype(BF16))
    send_g.start()
    for j in range(n):
        store(updated.at[j], updated_out.at[j, 0])

    @pl.when(odd == 1)
    def _():
        send_k.wait_recv()

    send_g.wait_recv()
    for t in range(half):
        mine, other = g_own[odd * half + t], g_other[t]
        lower = jnp.where(odd == 0, mine, other)
        upper = jnp.where(odd == 0, other, mine)
        k_lower, k_upper = keep_k[t, 0], keep_k[t, 1]
        for c in range(2):
            part = slice(c * size, (c + 1) * size)
            coarse[t, c, :size, :] = cat(1, lower[:, part], k_lower[:, part])
            coarse[t, c, size:, :] = cat(1, k_upper[:, part], upper[:, part])
    store(coarse, coarse_out.at[:, 0])

    send_fac_x.wait_recv()
    for copy in send_fac_y:
        copy.wait_recv()
    for copy in [send_par_x, send_par_y, send_w_x, send_g, send_fac_x, *send_w_y, *send_fac_y]:
        copy.wait_send()

    @pl.when(odd == 1)
    def _():
        send_extra.wait_send()

    @pl.when(odd == 0)
    def _():
        send_k.wait_send()

    for copy in outs:
        copy.wait()


def local(self_block, coupling, skeleton, redundant, interp, pivot, pivot_inverse):
    n, _, _, points, _ = self_block.shape
    size, half = skeleton.shape[2], n // 2
    vmem = pltpu.VMEM
    return pl.pallas_call(
        kernel,
        out_shape=(
            jax.ShapeDtypeStruct((n, 1, 5, 2, size, points), BF16),
            jax.ShapeDtypeStruct((n, 1, 2, points, points), BF16),
            jax.ShapeDtypeStruct((half, 1, 2, points, points), BF16),
        ),
        in_specs=[pl.BlockSpec(memory_space=pl.ANY)] * 7,
        out_specs=(pl.BlockSpec(memory_space=pl.ANY),) * 3,
        scratch_shapes=[
            vmem((n, 2, points, points), BF16),
            vmem((n, 4, 2, points, points), BF16),
            vmem((n, 1, size), jnp.int32),
            vmem((n, 1, size), jnp.int32),
            vmem((n, 2, size, size), BF16),
            vmem((n, 1, size), jnp.int32),
            vmem((n, 2, size, size), BF16),
            vmem((n, size, points), BF16),
            vmem((n, 3 * size, points), BF16),
            vmem((3 * size, points), BF16),
            vmem((n, 3 * size, points), BF16),
            vmem((n, 2 * size, points), BF16),
            vmem((n, 2 * size, points), BF16),
            vmem((n, 5, 2, size, points), BF16),
            vmem((n, 2 * points, points), F32),
            vmem((2 * points, points), BF16),
            vmem((n, 2 * points, points), BF16),
            vmem((2 * points, points), BF16),
            vmem((n, 2 * points, points), BF16),
            vmem((n, 2 * size, 2 * points), F32),
            vmem((n, 2, size, 2 * size), BF16),
            vmem((n, size, 2 * size), BF16),
            vmem((half, size, 2 * size), BF16),
            vmem((n, 2, points, points), BF16),
            vmem((half, 2, points, points), BF16),
            pltpu.SemaphoreType.DMA((5 + 2 * n,)),
            pltpu.SemaphoreType.DMA((7 + 2 * n,)),
            pltpu.SemaphoreType.DMA((7 + 2 * n,)),
            pltpu.SemaphoreType.DMA((5 * n,)),
        ],
        compiler_params=pltpu.CompilerParams(
            collective_id=0, has_side_effects=True, vmem_limit_bytes=24 * 2**20
        ),
    )(self_block, coupling, skeleton, redundant, interp, pivot, pivot_inverse)


def solution(mesh):
    box = P("gx", "gy", None, None, None)
    wide = P("gx", "gy", None, None, None, None)
    index = P("gx", "gy", None)
    return jax.shard_map(
        local,
        mesh=mesh,
        in_specs=(box, wide, index, index, box, index, box),
        out_specs=(wide, box, box),
        check_vma=False,
    )
```

```python
import jax
import jax.numpy as jnp
from jax import lax
from jax.experimental import pallas as pl
from jax.experimental.pallas import tpu as pltpu
from jax.sharding import PartitionSpec as P

MESH = pl.DeviceIdType.MESH
BF16, F32 = jnp.bfloat16, jnp.float32


def dot(left_op, right_op):
    return jnp.dot(left_op, right_op, preferred_element_type=F32)


def dot_nt(left_op, right_op):
    return lax.dot_general(left_op, right_op, (((1,), (1,)), ((), ())), preferred_element_type=F32)


def cat(axis, *parts):
    return jnp.concatenate(parts, axis)


def beside(ref, *index):
    return cat(1, ref[(*index, 0)], ref[(*index, 1)])


def above(ref, *index):
    return cat(0, ref[(*index, 0)], ref[(*index, 1)])


def folded(wide):
    half = wide.shape[1] // 2
    return cat(0, wide[:, :half], wide[:, half:])


def paired(tall):
    half = tall.shape[0] // 2
    return cat(1, tall[:half], tall[half:])


def make_params(par, pick, skel, red, interp, pivot, inverse, j):
    points, size = pick.shape[2], skel.shape[2]
    ids = lax.broadcasted_iota(jnp.int32, (points, size), 0)
    skel_t = jnp.where(ids == skel[j], 1.0, 0.0)
    red_t = jnp.where(ids == red[j], 1.0, 0.0)
    order = jnp.where(ids[:size] == pivot[j], 1.0, 0.0).astype(BF16)
    spread = dot(skel_t.astype(BF16), beside(interp, j))
    q_t = cat(1, red_t, jnp.zeros_like(red_t)) - spread
    par[j, 0 : 2 * size, :] = q_t.T.astype(BF16)
    turned = dot_nt(above(inverse, j), order).astype(BF16)
    par[j, 2 * size : 3 * size, :] = paired(turned)
    pick[j] = cat(1, skel_t, red_t).T[:size].astype(BF16)


def read_params(block):
    size = block.shape[0] // 3
    q_re, q_im, inv = block[:size], block[size : 2 * size], block[2 * size :]
    real_row, imag_row = cat(1, q_re, -q_im), cat(1, q_im, q_re)
    q_mix = cat(0, real_row, imag_row)
    e_mix = cat(0, real_row, -imag_row, imag_row, real_row)
    inv_re, inv_im = inv[:, :size], inv[:, size:]
    inv_mix = cat(0, cat(1, inv_re, -inv_im), cat(1, inv_im, inv_re))
    return q_mix, e_mix, inv_mix


def factors(params, right_op):
    q_mix, _, inv_mix = params
    return dot(inv_mix, dot(q_mix, right_op).astype(BF16)).astype(BF16)


def kernel(
    self_hbm, coup_hbm, skel_hbm, red_hbm, interp_hbm, pivot_hbm, inverse_hbm,
    factor_out, updated_out, coarse_out,
    own, coup, skel, red, interp, pivot, inverse,
    pick, par, par_x, par_y, extra, extra_y, fac, acc, w_send_x, w_send_y, w_x, w_y,
    self_term, keep_k, g_own, g_other, updated, coarse,
    in_sem, send_sem, recv_sem, out_sem,
):
    n, points = own.shape[0], own.shape[2]
    half, size = n // 2, skel.shape[2]
    gx, gy = lax.axis_index("gx"), lax.axis_index("gy")
    nx, ny = lax.axis_size("gx"), lax.axis_size("gy")
    x_next, x_back = {"gx": lax.rem(gx + 1, nx)}, {"gx": lax.rem(gx + nx - 1, nx)}
    y_next, y_back = {"gy": lax.rem(gy + 1, ny)}, {"gy": lax.rem(gy + ny - 1, ny)}
    odd = lax.rem(gy, 2)
    partner = {"gy": gy + 1 - 2 * odd}

    barrier = pltpu.get_barrier_semaphore()
    for device in (x_next, x_back, y_next, y_back):
        pl.semaphore_signal(barrier, inc=1, device_id=device, device_id_type=MESH)

    def load(source, target, at):
        copy = pltpu.make_async_copy(source, target, in_sem.at[at])
        copy.start()
        return copy

    small = [
        load(skel_hbm, skel, 0),
        load(red_hbm, red, 1),
        load(interp_hbm.at[:, 0], interp, 2),
        load(pivot_hbm, pivot, 3),
        load(inverse_hbm.at[:, 0], inverse, 4),
    ]
    large = []
    for j in range(n):
        large.append(
            (
                load(coup_hbm.at[j, 0], coup.at[j], 5 + 2 * j),
                load(self_hbm.at[j, 0], own.at[j], 6 + 2 * j),
            )
        )

    def remote(source, target, at, device):
        return pltpu.make_async_remote_copy(
            src_ref=source, dst_ref=target, send_sem=send_sem.at[at],
            recv_sem=recv_sem.at[at], device_id=device, device_id_type=MESH,
        )

    outs = []

    def store(source, target):
        copy = pltpu.make_async_copy(source, target, out_sem.at[len(outs)])
        copy.start()
        outs.append(copy)

    send_par_x = remote(par.at[0], par_x, 0, x_back)
    send_par_y = remote(par, par_y, 1, y_back)
    send_extra = remote(extra, extra_y, 2, y_back)
    send_w_x = remote(w_send_x, w_x, 3, x_next)
    send_k = remote(keep_k.at[pl.ds(half, half)], keep_k.at[pl.ds(0, half)], 4, partner)
    send_g = remote(g_own.at[pl.ds((1 - odd) * half, half)], g_other, 5, partner)
    send_fac_x = remote(fac.at[n - 1, 1], factor_out.at[0, 0, 1], 6, x_next)
    send_w_y = [remote(w_send_y.at[j], w_y.at[j], 7 + 2 * j, y_next) for j in range(n)]
    send_fac_y = [
        remote(fac.at[j, 3], factor_out.at[j, 0, 3], 8 + 2 * j, y_next) for j in range(n)
    ]

    def put_factor(j, k, value):
        fac[j, k] = value.reshape(2, size, points)

    for copy in small:
        copy.wait()
    for j in range(n):
        make_params(par, pick, skel, red, interp, pivot, inverse, j)
    pl.semaphore_wait(barrier, 4)
    send_par_y.start()
    send_par_x.start()

    for j in range(n):
        for copy in large[j]:
            copy.wait()
    params = [read_params(par[j]) for j in range(n)]
    w_right = []
    for j in range(n):
        right_ops = cat(1, above(coup, j, 2), above(coup, j, 0), above(own, j))
        made = factors(params[j], right_ops)
        f_up, f_right, f_own = (made[:, k * points : (k + 1) * points] for k in range(3))
        put_factor(j, 4, f_up)
        put_factor(j, 2, f_right)
        put_factor(j, 0, f_own)
        own_rows = dot(pick[j], beside(own, j)).astype(BF16)
        left_ops = cat(0, beside(coup, j, 3), beside(coup, j, 1), own_rows)
        ends = dot_nt(left_ops, params[j][1]).astype(BF16)
        w_send_y[j] = dot(folded(ends[:points]), f_up).astype(BF16)
        send_w_y[j].start()
        w_right.append(dot(folded(ends[points : 2 * points]), f_right))
        if j == n - 1:
            w_send_x[...] = w_right[j].astype(BF16)
            send_w_x.start()
        e_mix = folded(ends[2 * points :])
        self_term[j] = dot(e_mix, cat(1, f_own, f_up))
        extra[j, :size, :] = cat(1, e_mix[:size, :size], e_mix[size:, :size])
        extra[j, size:, :] = pick[j]
        acc[j] = above(own, j).astype(F32)
        if j > 0:
            acc[j] = acc[j] - w_right[j - 1]

    @pl.when(odd == 1)
    def _():
        send_extra.start()

    for j in range(n):
        for k in (0, 2, 4):
            store(fac.at[j, k], factor_out.at[j, 0, k])

    def from_next(next_params, j, k):
        made = factors(next_params, above(coup, j, k))
        put_factor(j, k, made)
        ends = dot_nt(beside(coup, j, k - 1), next_params[1]).astype(BF16)
        return made, dot(folded(ends), made)

    for j in range(n - 1):
        acc[j] = acc[j] - from_next(params[j + 1], j, 1)[1]
        store(fac.at[j, 1], factor_out.at[j + 1, 0, 1])
    send_par_y.wait_recv()
    for j in range(n):
        acc[j] = acc[j] - from_next(read_params(par_y[j]), j, 3)[1]
        send_fac_y[j].start()
    send_par_x.wait_recv()
    acc[n - 1] = acc[n - 1] - from_next(read_params(par_x[...]), n - 1, 1)[1]
    send_fac_x.start()

    @pl.when(odd == 0)
    def _():
        send_extra.wait_recv()
        for j in reversed(range(n)):
            lower_pick, upper_pick = pick[j], extra_y[j, size:, :]
            rows = folded(dot(lower_pick, beside(coup, j, 2))) - self_term[j, :, points:]
            keep_k[j, 0] = paired(dot_nt(rows.astype(BF16), upper_pick).astype(BF16))
            end = extra_y[j, :size, :]
            e_re, e_im = end[:, :size], end[:, size:]
            e_mix = cat(0, cat(1, e_re, -e_im), cat(1, e_im, e_re))
            upper_factor = above(fac, j, 3)
            rows = folded(dot(upper_pick, beside(coup, j, 3))) - dot(e_mix, upper_factor)
            keep_k[j, 1] = paired(dot_nt(rows.astype(BF16), lower_pick).astype(BF16))
        send_k.start()

    send_w_x.wait_recv()
    for j in range(n):
        send_w_y[j].wait_recv()
    for j in range(n):
        total = acc[j] - w_y[j].astype(F32)
        if j == 0:
            total = total - w_x[...].astype(F32)
        rounded = total.astype(BF16)
        rest = (total - rounded.astype(F32)).astype(BF16)
        updated[j] = rounded.reshape(2, points, points)
        rows = dot(pick[j], cat(1, paired(rounded), paired(rest)))
        rows = rows[:, : 2 * points] + rows[:, 2 * points :]
        rows = (folded(rows) - self_term[j, :, :points]).astype(BF16)
        g_own[j] = paired(dot_nt(rows, pick[j]).astype(BF16))
    send_g.start()
    for j in range(n):
        store(updated.at[j], updated_out.at[j, 0])

    @pl.when(odd == 1)
    def _():
        send_k.wait_recv()

    send_g.wait_recv()
    for t in range(half):
        mine, other = g_own[odd * half + t], g_other[t]
        lower = jnp.where(odd == 0, mine, other)
        upper = jnp.where(odd == 0, other, mine)
        k_lower, k_upper = keep_k[t, 0], keep_k[t, 1]
        for c in range(2):
            part = slice(c * size, (c + 1) * size)
            coarse[t, c, :size, :] = cat(1, lower[:, part], k_lower[:, part])
            coarse[t, c, size:, :] = cat(1, k_upper[:, part], upper[:, part])
    store(coarse, coarse_out.at[:, 0])

    send_fac_x.wait_recv()
    for copy in send_fac_y:
        copy.wait_recv()
    for copy in [send_par_x, send_par_y, send_w_x, send_g, send_fac_x, *send_w_y, *send_fac_y]:
        copy.wait_send()

    @pl.when(odd == 1)
    def _():
        send_extra.wait_send()

    @pl.when(odd == 0)
    def _():
        send_k.wait_send()

    for copy in outs:
        copy.wait()


def hand_over(*refs):
    sources, targets, sem = refs[:3], refs[3:6], refs[6]
    copies = [
        pltpu.make_async_copy(source, target, sem.at[at])
        for at, (source, target) in enumerate(zip(sources, targets))
    ]
    for copy in copies:
        copy.start()
    for copy in copies:
        copy.wait()


def local(self_block, coupling, skeleton, redundant, interp, pivot, pivot_inverse):
    n, _, _, points, _ = self_block.shape
    size, half = skeleton.shape[2], n // 2
    vmem = pltpu.VMEM
    shapes = (
        jax.ShapeDtypeStruct((n, 1, 5, 2, size, points), BF16),
        jax.ShapeDtypeStruct((n, 1, 2, points, points), BF16),
        jax.ShapeDtypeStruct((half, 1, 2, points, points), BF16),
    )
    made = pl.pallas_call(
        kernel,
        out_shape=shapes,
        in_specs=[pl.BlockSpec(memory_space=pl.ANY)] * 7,
        out_specs=(pl.BlockSpec(memory_space=pl.ANY),) * 3,
        scratch_shapes=[
            vmem((n, 2, points, points), BF16),
            vmem((n, 4, 2, points, points), BF16),
            vmem((n, 1, size), jnp.int32),
            vmem((n, 1, size), jnp.int32),
            vmem((n, 2, size, size), BF16),
            vmem((n, 1, size), jnp.int32),
            vmem((n, 2, size, size), BF16),
            vmem((n, size, points), BF16),
            vmem((n, 3 * size, points), BF16),
            vmem((3 * size, points), BF16),
            vmem((n, 3 * size, points), BF16),
            vmem((n, 2 * size, points), BF16),
            vmem((n, 2 * size, points), BF16),
            vmem((n, 5, 2, size, points), BF16),
            vmem((n, 2 * points, points), F32),
            vmem((2 * points, points), BF16),
            vmem((n, 2 * points, points), BF16),
            vmem((2 * points, points), BF16),
            vmem((n, 2 * points, points), BF16),
            vmem((n, 2 * size, 2 * points), F32),
            vmem((n, 2, size, 2 * size), BF16),
            vmem((n, size, 2 * size), BF16),
            vmem((half, size, 2 * size), BF16),
            vmem((n, 2, points, points), BF16),
            vmem((half, 2, points, points), BF16),
            pltpu.SemaphoreType.DMA((5 + 2 * n,)),
            pltpu.SemaphoreType.DMA((7 + 2 * n,)),
            pltpu.SemaphoreType.DMA((7 + 2 * n,)),
            pltpu.SemaphoreType.DMA((5 * n,)),
        ],
        compiler_params=pltpu.CompilerParams(
            collective_id=0, has_side_effects=True, vmem_limit_bytes=62 * 2**20
        ),
    )(self_block, coupling, skeleton, redundant, interp, pivot, pivot_inverse)
    return pl.pallas_call(
        hand_over,
        out_shape=shapes,
        in_specs=[pl.BlockSpec(memory_space=pl.ANY)] * 3,
        out_specs=(pl.BlockSpec(memory_space=pltpu.HBM),) * 3,
        scratch_shapes=[pltpu.SemaphoreType.DMA((3,))],
        compiler_params=pltpu.CompilerParams(vmem_limit_bytes=62 * 2**20),
    )(*made)


def solution(mesh):
    box = P("gx", "gy", None, None, None)
    wide = P("gx", "gy", None, None, None, None)
    index = P("gx", "gy", None)
    return jax.shard_map(
        local,
        mesh=mesh,
        in_specs=(box, wide, index, index, box, index, box),
        out_specs=(wide, box, box),
        check_vma=False,
    )
```

```python
import jax
import jax.numpy as jnp
from jax import lax
from jax.experimental import pallas as pl
from jax.experimental.pallas import tpu as pltpu
from jax.sharding import PartitionSpec as P

MESH = pl.DeviceIdType.MESH
BF16, F32 = jnp.bfloat16, jnp.float32


def dot(left_op, right_op):
    return jnp.dot(left_op, right_op, preferred_element_type=F32)


def dot_nt(left_op, right_op):
    return lax.dot_general(left_op, right_op, (((1,), (1,)), ((), ())), preferred_element_type=F32)


def cat(axis, *parts):
    return jnp.concatenate(parts, axis)


def beside(ref, *index):
    return cat(1, ref[(*index, 0)], ref[(*index, 1)])


def above(ref, *index):
    return cat(0, ref[(*index, 0)], ref[(*index, 1)])


def folded(wide):
    half = wide.shape[1] // 2
    return cat(0, wide[:, :half], wide[:, half:])


def paired(tall):
    half = tall.shape[0] // 2
    return cat(1, tall[:half], tall[half:])


def make_params(par, pick, skel, red, interp, pivot, inverse, j):
    points, size = pick.shape[2], skel.shape[2]
    ids = lax.broadcasted_iota(jnp.int32, (points, size), 0)
    skel_t = jnp.where(ids == skel[j], 1.0, 0.0)
    red_t = jnp.where(ids == red[j], 1.0, 0.0)
    order = jnp.where(ids[:size] == pivot[j], 1.0, 0.0).astype(BF16)
    spread = dot(skel_t.astype(BF16), beside(interp, j))
    q_t = cat(1, red_t, jnp.zeros_like(red_t)) - spread
    par[j, 0 : 2 * size, :] = q_t.T.astype(BF16)
    turned = dot_nt(above(inverse, j), order).astype(BF16)
    par[j, 2 * size : 3 * size, :] = paired(turned)
    pick[j] = cat(1, skel_t, red_t).T[:size].astype(BF16)


def read_params(block):
    size = block.shape[0] // 3
    q_re, q_im, inv = block[:size], block[size : 2 * size], block[2 * size :]
    real_row, imag_row = cat(1, q_re, -q_im), cat(1, q_im, q_re)
    q_mix = cat(0, real_row, imag_row)
    e_mix = cat(0, real_row, -imag_row, imag_row, real_row)
    inv_re, inv_im = inv[:, :size], inv[:, size:]
    inv_mix = cat(0, cat(1, inv_re, -inv_im), cat(1, inv_im, inv_re))
    return q_mix, e_mix, inv_mix


def factors(params, right_op):
    q_mix, _, inv_mix = params
    return dot(inv_mix, dot(q_mix, right_op).astype(BF16)).astype(BF16)


def kernel(
    self_hbm, coup_hbm, skel_hbm, red_hbm, interp_hbm, pivot_hbm, inverse_hbm,
    factor_out, updated_out, coarse_out,
    own, coup, skel, red, interp, pivot, inverse,
    pick, par, par_x, par_y, extra, extra_y, fac, acc, w_send_x, w_send_y, w_x, w_y,
    self_term, keep_k, g_own, g_other, updated, coarse,
    in_sem, send_sem, recv_sem, out_sem,
):
    n, points = own.shape[0], own.shape[2]
    half, size = n // 2, skel.shape[2]
    gx, gy = lax.axis_index("gx"), lax.axis_index("gy")
    nx, ny = lax.axis_size("gx"), lax.axis_size("gy")
    x_next, x_back = {"gx": lax.rem(gx + 1, nx)}, {"gx": lax.rem(gx + nx - 1, nx)}
    y_next, y_back = {"gy": lax.rem(gy + 1, ny)}, {"gy": lax.rem(gy + ny - 1, ny)}
    odd = lax.rem(gy, 2)
    partner = {"gy": gy + 1 - 2 * odd}

    barrier = pltpu.get_barrier_semaphore()
    for device in (x_next, x_back, y_next, y_back):
        pl.semaphore_signal(barrier, inc=1, device_id=device, device_id_type=MESH)

    def load(source, target, at):
        copy = pltpu.make_async_copy(source, target, in_sem.at[at])
        copy.start()
        return copy

    small = [
        load(skel_hbm, skel, 0),
        load(red_hbm, red, 1),
        load(interp_hbm.at[:, 0], interp, 2),
        load(pivot_hbm, pivot, 3),
        load(inverse_hbm.at[:, 0], inverse, 4),
    ]
    large = []
    for j in range(n):
        large.append(
            (
                load(coup_hbm.at[j, 0], coup.at[j], 5 + 2 * j),
                load(self_hbm.at[j, 0], own.at[j], 6 + 2 * j),
            )
        )

    def remote(source, target, at, device):
        return pltpu.make_async_remote_copy(
            src_ref=source, dst_ref=target, send_sem=send_sem.at[at],
            recv_sem=recv_sem.at[at], device_id=device, device_id_type=MESH,
        )

    outs = []

    def store(source, target):
        copy = pltpu.make_async_copy(source, target, out_sem.at[len(outs)])
        copy.start()
        outs.append(copy)

    send_par_x = remote(par.at[0], par_x, 0, x_back)
    send_par_y = remote(par, par_y, 1, y_back)
    send_extra = remote(extra, extra_y, 2, y_back)
    send_w_x = remote(w_send_x, w_x, 3, x_next)
    send_k = remote(keep_k.at[pl.ds(half, half)], keep_k.at[pl.ds(0, half)], 4, partner)
    send_g = remote(g_own.at[pl.ds((1 - odd) * half, half)], g_other, 5, partner)
    send_fac_x = remote(fac.at[n - 1, 1], factor_out.at[0, 0, 1], 6, x_next)
    send_w_y = [remote(w_send_y.at[j], w_y.at[j], 7 + 2 * j, y_next) for j in range(n)]
    send_fac_y = [
        remote(fac.at[j, 3], factor_out.at[j, 0, 3], 8 + 2 * j, y_next) for j in range(n)
    ]

    def put_factor(j, k, value):
        fac[j, k] = value.reshape(2, size, points)

    for copy in small:
        copy.wait()
    for j in range(n):
        make_params(par, pick, skel, red, interp, pivot, inverse, j)
    pl.semaphore_wait(barrier, 4)
    send_par_y.start()
    send_par_x.start()

    for j in range(n):
        for copy in large[j]:
            copy.wait()
    params = [read_params(par[j]) for j in range(n)]
    w_right = []
    for j in range(n):
        right_ops = cat(1, above(coup, j, 2), above(coup, j, 0), above(own, j))
        made = factors(params[j], right_ops)
        f_up, f_right, f_own = (made[:, k * points : (k + 1) * points] for k in range(3))
        put_factor(j, 4, f_up)
        put_factor(j, 2, f_right)
        put_factor(j, 0, f_own)
        own_rows = dot(pick[j], beside(own, j)).astype(BF16)
        left_ops = cat(0, beside(coup, j, 3), beside(coup, j, 1), own_rows)
        ends = dot_nt(left_ops, params[j][1]).astype(BF16)
        w_send_y[j] = dot(folded(ends[:points]), f_up).astype(BF16)
        send_w_y[j].start()
        w_right.append(dot(folded(ends[points : 2 * points]), f_right))
        if j == n - 1:
            w_send_x[...] = w_right[j].astype(BF16)
            send_w_x.start()
        e_mix = folded(ends[2 * points :])
        self_term[j] = dot(e_mix, cat(1, f_own, f_up))
        extra[j, :size, :] = cat(1, e_mix[:size, :size], e_mix[size:, :size])
        extra[j, size:, :] = pick[j]
        acc[j] = above(own, j).astype(F32)
        if j > 0:
            acc[j] = acc[j] - w_right[j - 1]

    @pl.when(odd == 1)
    def _():
        send_extra.start()

    for j in range(n):
        for k in (0, 2, 4):
            store(fac.at[j, k], factor_out.at[j, 0, k])

    def from_next(next_params, j, k):
        made = factors(next_params, above(coup, j, k))
        put_factor(j, k, made)
        ends = dot_nt(beside(coup, j, k - 1), next_params[1]).astype(BF16)
        return made, dot(folded(ends), made)

    for j in range(n - 1):
        acc[j] = acc[j] - from_next(params[j + 1], j, 1)[1]
        store(fac.at[j, 1], factor_out.at[j + 1, 0, 1])
    send_par_y.wait_recv()
    for j in range(n):
        acc[j] = acc[j] - from_next(read_params(par_y[j]), j, 3)[1]
        send_fac_y[j].start()
    send_par_x.wait_recv()
    acc[n - 1] = acc[n - 1] - from_next(read_params(par_x[...]), n - 1, 1)[1]
    send_fac_x.start()

    @pl.when(odd == 0)
    def _():
        send_extra.wait_recv()
        for j in reversed(range(n)):
            lower_pick, upper_pick = pick[j], extra_y[j, size:, :]
            rows = folded(dot(lower_pick, beside(coup, j, 2))) - self_term[j, :, points:]
            keep_k[j, 0] = paired(dot_nt(rows.astype(BF16), upper_pick).astype(BF16))
            end = extra_y[j, :size, :]
            e_re, e_im = end[:, :size], end[:, size:]
            e_mix = cat(0, cat(1, e_re, -e_im), cat(1, e_im, e_re))
            upper_factor = above(fac, j, 3)
            rows = folded(dot(upper_pick, beside(coup, j, 3))) - dot(e_mix, upper_factor)
            keep_k[j, 1] = paired(dot_nt(rows.astype(BF16), lower_pick).astype(BF16))
        send_k.start()

    send_w_x.wait_recv()
    for j in range(n):
        send_w_y[j].wait_recv()
    for j in range(n):
        total = acc[j] - w_y[j].astype(F32)
        if j == 0:
            total = total - w_x[...].astype(F32)
        rounded = total.astype(BF16)
        rest = (total - rounded.astype(F32)).astype(BF16)
        updated[j] = rounded.reshape(2, points, points)
        rows = dot(pick[j], cat(1, paired(rounded), paired(rest)))
        rows = rows[:, : 2 * points] + rows[:, 2 * points :]
        rows = (folded(rows) - self_term[j, :, :points]).astype(BF16)
        g_own[j] = paired(dot_nt(rows, pick[j]).astype(BF16))
    send_g.start()
    for j in range(n):
        store(updated.at[j], updated_out.at[j, 0])

    @pl.when(odd == 1)
    def _():
        send_k.wait_recv()

    send_g.wait_recv()
    for t in range(half):
        mine, other = g_own[odd * half + t], g_other[t]
        lower = jnp.where(odd == 0, mine, other)
        upper = jnp.where(odd == 0, other, mine)
        k_lower, k_upper = keep_k[t, 0], keep_k[t, 1]
        for c in range(2):
            part = slice(c * size, (c + 1) * size)
            coarse[t, c, :size, :] = cat(1, lower[:, part], k_lower[:, part])
            coarse[t, c, size:, :] = cat(1, k_upper[:, part], upper[:, part])
    store(coarse, coarse_out.at[:, 0])

    send_fac_x.wait_recv()
    for copy in send_fac_y:
        copy.wait_recv()
    for copy in [send_par_x, send_par_y, send_w_x, send_g, send_fac_x, *send_w_y, *send_fac_y]:
        copy.wait_send()

    @pl.when(odd == 1)
    def _():
        send_extra.wait_send()

    @pl.when(odd == 0)
    def _():
        send_k.wait_send()

    for copy in outs:
        copy.wait()


def hand_over(*refs):
    sources, targets, sem = refs[:3], refs[3:6], refs[6]
    copies = [
        pltpu.make_async_copy(source, target, sem.at[at])
        for at, (source, target) in enumerate(zip(sources, targets))
    ]
    for copy in copies:
        copy.start()
    for copy in copies:
        copy.wait()


def local(self_block, coupling, skeleton, redundant, interp, pivot, pivot_inverse):
    n, _, _, points, _ = self_block.shape
    size, half = skeleton.shape[2], n // 2
    vmem = pltpu.VMEM
    shapes = (
        jax.ShapeDtypeStruct((n, 1, 5, 2, size, points), BF16),
        jax.ShapeDtypeStruct((n, 1, 2, points, points), BF16),
        jax.ShapeDtypeStruct((half, 1, 2, points, points), BF16),
    )
    made = pl.pallas_call(
        kernel,
        out_shape=tuple(pltpu.VMEM(shape.shape, shape.dtype) for shape in shapes),
        in_specs=[pl.BlockSpec(memory_space=pl.ANY)] * 7,
        out_specs=(pl.BlockSpec(memory_space=pl.ANY),) * 3,
        scratch_shapes=[
            vmem((n, 2, points, points), BF16),
            vmem((n, 4, 2, points, points), BF16),
            vmem((n, 1, size), jnp.int32),
            vmem((n, 1, size), jnp.int32),
            vmem((n, 2, size, size), BF16),
            vmem((n, 1, size), jnp.int32),
            vmem((n, 2, size, size), BF16),
            vmem((n, size, points), BF16),
            vmem((n, 3 * size, points), BF16),
            vmem((3 * size, points), BF16),
            vmem((n, 3 * size, points), BF16),
            vmem((n, 2 * size, points), BF16),
            vmem((n, 2 * size, points), BF16),
            vmem((n, 5, 2, size, points), BF16),
            vmem((n, 2 * points, points), F32),
            vmem((2 * points, points), BF16),
            vmem((n, 2 * points, points), BF16),
            vmem((2 * points, points), BF16),
            vmem((n, 2 * points, points), BF16),
            vmem((n, 2 * size, 2 * points), F32),
            vmem((n, 2, size, 2 * size), BF16),
            vmem((n, size, 2 * size), BF16),
            vmem((half, size, 2 * size), BF16),
            vmem((n, 2, points, points), BF16),
            vmem((half, 2, points, points), BF16),
            pltpu.SemaphoreType.DMA((5 + 2 * n,)),
            pltpu.SemaphoreType.DMA((7 + 2 * n,)),
            pltpu.SemaphoreType.DMA((7 + 2 * n,)),
            pltpu.SemaphoreType.DMA((5 * n,)),
        ],
        compiler_params=pltpu.CompilerParams(
            collective_id=0, has_side_effects=True, vmem_limit_bytes=62 * 2**20
        ),
    )(self_block, coupling, skeleton, redundant, interp, pivot, pivot_inverse)
    return pl.pallas_call(
        hand_over,
        out_shape=shapes,
        in_specs=[pl.BlockSpec(memory_space=pl.ANY)] * 3,
        out_specs=(pl.BlockSpec(memory_space=pltpu.HBM),) * 3,
        scratch_shapes=[pltpu.SemaphoreType.DMA((3,))],
        compiler_params=pltpu.CompilerParams(vmem_limit_bytes=2**20),
    )(*made)


def solution(mesh):
    box = P("gx", "gy", None, None, None)
    wide = P("gx", "gy", None, None, None, None)
    index = P("gx", "gy", None)
    return jax.shard_map(
        local,
        mesh=mesh,
        in_specs=(box, wide, index, index, box, index, box),
        out_specs=(wide, box, box),
        check_vma=False,
    )
```

```python
import jax
import jax.numpy as jnp
from jax import lax
from jax.experimental import pallas as pl
from jax.experimental.pallas import tpu as pltpu
from jax.sharding import PartitionSpec as P

MESH = pl.DeviceIdType.MESH
BF16, F32 = jnp.bfloat16, jnp.float32


def dot(left_op, right_op):
    return jnp.dot(left_op, right_op, preferred_element_type=F32)


def dot_nt(left_op, right_op):
    return lax.dot_general(left_op, right_op, (((1,), (1,)), ((), ())), preferred_element_type=F32)


def cat(axis, *parts):
    return jnp.concatenate(parts, axis)


def beside(ref, *index):
    return cat(1, ref[(*index, 0)], ref[(*index, 1)])


def above(ref, *index):
    return cat(0, ref[(*index, 0)], ref[(*index, 1)])


def folded(wide):
    half = wide.shape[1] // 2
    return cat(0, wide[:, :half], wide[:, half:])


def paired(tall):
    half = tall.shape[0] // 2
    return cat(1, tall[:half], tall[half:])


def make_params(par, pick, skel, red, interp, pivot, inverse, j):
    points, size = pick.shape[2], skel.shape[2]
    ids = lax.broadcasted_iota(jnp.int32, (points, size), 0)
    skel_t = jnp.where(ids == skel[j], 1.0, 0.0)
    red_t = jnp.where(ids == red[j], 1.0, 0.0)
    order = jnp.where(ids[:size] == pivot[j], 1.0, 0.0).astype(BF16)
    spread = dot(skel_t.astype(BF16), beside(interp, j))
    q_t = cat(1, red_t, jnp.zeros_like(red_t)) - spread
    par[j, 0 : 2 * size, :] = q_t.T.astype(BF16)
    turned = dot_nt(above(inverse, j), order).astype(BF16)
    par[j, 2 * size : 3 * size, :] = paired(turned)
    pick[j] = cat(1, skel_t, red_t).T[:size].astype(BF16)


def read_params(block):
    size = block.shape[0] // 3
    q_re, q_im, inv = block[:size], block[size : 2 * size], block[2 * size :]
    real_row, imag_row = cat(1, q_re, -q_im), cat(1, q_im, q_re)
    q_mix = cat(0, real_row, imag_row)
    e_mix = cat(0, real_row, -imag_row, imag_row, real_row)
    inv_re, inv_im = inv[:, :size], inv[:, size:]
    inv_mix = cat(0, cat(1, inv_re, -inv_im), cat(1, inv_im, inv_re))
    return q_mix, e_mix, inv_mix


def factors(params, right_op):
    q_mix, _, inv_mix = params
    return dot(inv_mix, dot(q_mix, right_op).astype(BF16)).astype(BF16)


def kernel(
    self_hbm, coup_hbm, skel_hbm, red_hbm, interp_hbm, pivot_hbm, inverse_hbm,
    factor_out, updated_out, coarse_out,
    own, coup, skel, red, interp, pivot, inverse,
    pick, par, par_x, par_y, extra, extra_y, fac, acc, w_send_x, w_send_y, w_x, w_y,
    self_term, keep_k, g_own, g_other, updated, coarse,
    in_sem, send_sem, recv_sem, out_sem,
):
    n, points = own.shape[0], own.shape[2]
    half, size = n // 2, skel.shape[2]
    gx, gy = lax.axis_index("gx"), lax.axis_index("gy")
    nx, ny = lax.axis_size("gx"), lax.axis_size("gy")
    x_next, x_back = {"gx": lax.rem(gx + 1, nx)}, {"gx": lax.rem(gx + nx - 1, nx)}
    y_next, y_back = {"gy": lax.rem(gy + 1, ny)}, {"gy": lax.rem(gy + ny - 1, ny)}
    odd = lax.rem(gy, 2)
    partner = {"gy": gy + 1 - 2 * odd}

    barrier = pltpu.get_barrier_semaphore()
    for device in (x_next, x_back, y_next, y_back):
        pl.semaphore_signal(barrier, inc=1, device_id=device, device_id_type=MESH)

    def load(source, target, at):
        copy = pltpu.make_async_copy(source, target, in_sem.at[at])
        copy.start()
        return copy

    small = [
        load(skel_hbm, skel, 0),
        load(red_hbm, red, 1),
        load(interp_hbm.at[:, 0], interp, 2),
        load(pivot_hbm, pivot, 3),
        load(inverse_hbm.at[:, 0], inverse, 4),
    ]
    large = []
    for j in range(n):
        large.append(
            (
                load(coup_hbm.at[j, 0], coup.at[j], 5 + 2 * j),
                load(self_hbm.at[j, 0], own.at[j], 6 + 2 * j),
            )
        )

    def remote(source, target, at, device):
        return pltpu.make_async_remote_copy(
            src_ref=source, dst_ref=target, send_sem=send_sem.at[at],
            recv_sem=recv_sem.at[at], device_id=device, device_id_type=MESH,
        )

    outs = []

    def store(source, target):
        copy = pltpu.make_async_copy(source, target, out_sem.at[len(outs)])
        copy.start()
        outs.append(copy)

    send_par_x = remote(par.at[0], par_x, 0, x_back)
    send_par_y = remote(par, par_y, 1, y_back)
    send_extra = remote(extra, extra_y, 2, y_back)
    send_w_x = remote(w_send_x, w_x, 3, x_next)
    send_k = remote(keep_k.at[pl.ds(half, half)], keep_k.at[pl.ds(0, half)], 4, partner)
    send_g = remote(g_own.at[pl.ds((1 - odd) * half, half)], g_other, 5, partner)
    send_fac_x = remote(fac.at[n - 1, 1], factor_out.at[0, 0, 1], 6, x_next)
    send_w_y = [remote(w_send_y.at[j], w_y.at[j], 7 + 2 * j, y_next) for j in range(n)]
    send_fac_y = [
        remote(fac.at[j, 3], factor_out.at[j, 0, 3], 8 + 2 * j, y_next) for j in range(n)
    ]

    def put_factor(j, k, value):
        fac[j, k] = value.reshape(2, size, points)

    for copy in small:
        copy.wait()
    for j in range(n):
        make_params(par, pick, skel, red, interp, pivot, inverse, j)
    pl.semaphore_wait(barrier, 4)
    send_par_y.start()
    send_par_x.start()

    for pair in large:
        for copy in pair:
            copy.wait()
    params = [read_params(par[j]) for j in range(n)]
    made = [
        factors(params[j], cat(1, above(coup, j, 2), above(coup, j, 0), above(own, j)))
        for j in range(n)
    ]
    ends = [
        dot_nt(cat(0, beside(coup, j, 3), beside(coup, j, 1)), params[j][1]).astype(BF16)
        for j in range(n)
    ]
    f_up, f_right, f_own = (
        [made[j][:, k * points : (k + 1) * points] for j in range(n)] for k in range(3)
    )
    w_up = [dot(folded(ends[j][:points]), f_up[j]) for j in range(n)]
    w_right = [dot(folded(ends[j][points:]), f_right[j]) for j in range(n)]
    for j in range(n):
        w_send_y[j] = w_up[j].astype(BF16)
    w_send_x[...] = w_right[n - 1].astype(BF16)
    for copy in send_w_y:
        copy.start()
    send_w_x.start()

    def from_next(next_params, j, k):
        made = factors(next_params, above(coup, j, k))
        put_factor(j, k, made)
        ends = dot_nt(beside(coup, j, k - 1), next_params[1]).astype(BF16)
        return dot(folded(ends), made)

    for j in range(n):
        put_factor(j, 4, f_up[j])
        put_factor(j, 2, f_right[j])
        put_factor(j, 0, f_own[j])
        own_rows = dot(pick[j], beside(own, j)).astype(BF16)
        e_mix = folded(dot_nt(own_rows, params[j][1]).astype(BF16))
        self_term[j] = dot(e_mix, cat(1, f_own[j], f_up[j]))
        extra[j, :size, :] = cat(1, e_mix[:size, :size], e_mix[size:, :size])
        extra[j, size:, :] = pick[j]
        block = above(own, j).astype(F32)
        if j > 0:
            block = block - w_right[j - 1]
        if j < n - 1:
            block = block - from_next(params[j + 1], j, 1)
        acc[j] = block

    @pl.when(odd == 1)
    def _():
        send_extra.start()

    for j in range(n):
        for k in (0, 2, 4):
            store(fac.at[j, k], factor_out.at[j, 0, k])
    for j in range(n - 1):
        store(fac.at[j, 1], factor_out.at[j + 1, 0, 1])

    send_par_y.wait_recv()
    send_par_x.wait_recv()
    y_params = [read_params(par_y[j]) for j in range(n)]
    gained = [from_next(y_params[j], j, 3) for j in range(n)]
    gained[n - 1] = gained[n - 1] + from_next(read_params(par_x[...]), n - 1, 1)
    for j in range(n):
        acc[j] = acc[j] - gained[j]
    for copy in send_fac_y:
        copy.start()
    send_fac_x.start()

    @pl.when(odd == 0)
    def _():
        send_extra.wait_recv()
        for j in reversed(range(n)):
            lower_pick, upper_pick = pick[j], extra_y[j, size:, :]
            rows = folded(dot(lower_pick, beside(coup, j, 2))) - self_term[j, :, points:]
            keep_k[j, 0] = paired(dot_nt(rows.astype(BF16), upper_pick).astype(BF16))
            end = extra_y[j, :size, :]
            e_re, e_im = end[:, :size], end[:, size:]
            e_mix = cat(0, cat(1, e_re, -e_im), cat(1, e_im, e_re))
            upper_factor = above(fac, j, 3)
            rows = folded(dot(upper_pick, beside(coup, j, 3))) - dot(e_mix, upper_factor)
            keep_k[j, 1] = paired(dot_nt(rows.astype(BF16), lower_pick).astype(BF16))
        send_k.start()

    send_w_x.wait_recv()
    for j in range(n):
        send_w_y[j].wait_recv()
    for j in range(n):
        total = acc[j] - w_y[j].astype(F32)
        if j == 0:
            total = total - w_x[...].astype(F32)
        rounded = total.astype(BF16)
        rest = (total - rounded.astype(F32)).astype(BF16)
        updated[j] = rounded.reshape(2, points, points)
        rows = dot(pick[j], cat(1, paired(rounded), paired(rest)))
        rows = rows[:, : 2 * points] + rows[:, 2 * points :]
        rows = (folded(rows) - self_term[j, :, :points]).astype(BF16)
        g_own[j] = paired(dot_nt(rows, pick[j]).astype(BF16))
    send_g.start()
    for j in range(n):
        store(updated.at[j], updated_out.at[j, 0])

    @pl.when(odd == 1)
    def _():
        send_k.wait_recv()

    send_g.wait_recv()
    for t in range(half):
        mine, other = g_own[odd * half + t], g_other[t]
        lower = jnp.where(odd == 0, mine, other)
        upper = jnp.where(odd == 0, other, mine)
        k_lower, k_upper = keep_k[t, 0], keep_k[t, 1]
        for c in range(2):
            part = slice(c * size, (c + 1) * size)
            coarse[t, c, :size, :] = cat(1, lower[:, part], k_lower[:, part])
            coarse[t, c, size:, :] = cat(1, k_upper[:, part], upper[:, part])
    store(coarse, coarse_out.at[:, 0])

    send_fac_x.wait_recv()
    for copy in send_fac_y:
        copy.wait_recv()
    for copy in [send_par_x, send_par_y, send_w_x, send_g, send_fac_x, *send_w_y, *send_fac_y]:
        copy.wait_send()

    @pl.when(odd == 1)
    def _():
        send_extra.wait_send()

    @pl.when(odd == 0)
    def _():
        send_k.wait_send()

    for copy in outs:
        copy.wait()


def hand_over(*refs):
    sources, targets, sem = refs[:3], refs[3:6], refs[6]
    copies = [
        pltpu.make_async_copy(source, target, sem.at[at])
        for at, (source, target) in enumerate(zip(sources, targets))
    ]
    for copy in copies:
        copy.start()
    for copy in copies:
        copy.wait()


def local(self_block, coupling, skeleton, redundant, interp, pivot, pivot_inverse):
    n, _, _, points, _ = self_block.shape
    size, half = skeleton.shape[2], n // 2
    vmem = pltpu.VMEM
    shapes = (
        jax.ShapeDtypeStruct((n, 1, 5, 2, size, points), BF16),
        jax.ShapeDtypeStruct((n, 1, 2, points, points), BF16),
        jax.ShapeDtypeStruct((half, 1, 2, points, points), BF16),
    )
    made = pl.pallas_call(
        kernel,
        out_shape=tuple(pltpu.VMEM(shape.shape, shape.dtype) for shape in shapes),
        in_specs=[pl.BlockSpec(memory_space=pl.ANY)] * 7,
        out_specs=(pl.BlockSpec(memory_space=pl.ANY),) * 3,
        scratch_shapes=[
            vmem((n, 2, points, points), BF16),
            vmem((n, 4, 2, points, points), BF16),
            vmem((n, 1, size), jnp.int32),
            vmem((n, 1, size), jnp.int32),
            vmem((n, 2, size, size), BF16),
            vmem((n, 1, size), jnp.int32),
            vmem((n, 2, size, size), BF16),
            vmem((n, size, points), BF16),
            vmem((n, 3 * size, points), BF16),
            vmem((3 * size, points), BF16),
            vmem((n, 3 * size, points), BF16),
            vmem((n, 2 * size, points), BF16),
            vmem((n, 2 * size, points), BF16),
            vmem((n, 5, 2, size, points), BF16),
            vmem((n, 2 * points, points), F32),
            vmem((2 * points, points), BF16),
            vmem((n, 2 * points, points), BF16),
            vmem((2 * points, points), BF16),
            vmem((n, 2 * points, points), BF16),
            vmem((n, 2 * size, 2 * points), F32),
            vmem((n, 2, size, 2 * size), BF16),
            vmem((n, size, 2 * size), BF16),
            vmem((half, size, 2 * size), BF16),
            vmem((n, 2, points, points), BF16),
            vmem((half, 2, points, points), BF16),
            pltpu.SemaphoreType.DMA((5 + 2 * n,)),
            pltpu.SemaphoreType.DMA((7 + 2 * n,)),
            pltpu.SemaphoreType.DMA((7 + 2 * n,)),
            pltpu.SemaphoreType.DMA((5 * n,)),
        ],
        compiler_params=pltpu.CompilerParams(
            collective_id=0, has_side_effects=True, vmem_limit_bytes=62 * 2**20
        ),
    )(self_block, coupling, skeleton, redundant, interp, pivot, pivot_inverse)
    return pl.pallas_call(
        hand_over,
        out_shape=shapes,
        in_specs=[pl.BlockSpec(memory_space=pl.ANY)] * 3,
        out_specs=(pl.BlockSpec(memory_space=pltpu.HBM),) * 3,
        scratch_shapes=[pltpu.SemaphoreType.DMA((3,))],
        compiler_params=pltpu.CompilerParams(vmem_limit_bytes=2**20),
    )(*made)


def solution(mesh):
    box = P("gx", "gy", None, None, None)
    wide = P("gx", "gy", None, None, None, None)
    index = P("gx", "gy", None)
    return jax.shard_map(
        local,
        mesh=mesh,
        in_specs=(box, wide, index, index, box, index, box),
        out_specs=(wide, box, box),
        check_vma=False,
    )
```

```python
import jax
import jax.numpy as jnp
from jax import lax
from jax.experimental import pallas as pl
from jax.experimental.pallas import tpu as pltpu
from jax.sharding import PartitionSpec as P

MESH = pl.DeviceIdType.MESH
BF16, F32 = jnp.bfloat16, jnp.float32


def dot(left_op, right_op):
    return jnp.dot(left_op, right_op, preferred_element_type=F32)


def dot_nt(left_op, right_op):
    return lax.dot_general(left_op, right_op, (((1,), (1,)), ((), ())), preferred_element_type=F32)


def cat(axis, *parts):
    return jnp.concatenate(parts, axis)


def beside(ref, *index):
    return cat(1, ref[(*index, 0)], ref[(*index, 1)])


def above(ref, *index):
    return cat(0, ref[(*index, 0)], ref[(*index, 1)])


def folded(wide):
    half = wide.shape[1] // 2
    return cat(0, wide[:, :half], wide[:, half:])


def paired(tall):
    half = tall.shape[0] // 2
    return cat(1, tall[:half], tall[half:])


def make_params(par, pick, skel, red, interp, pivot, inverse, j):
    points, size = pick.shape[2], skel.shape[2]
    ids = lax.broadcasted_iota(jnp.int32, (points, size), 0)
    skel_t = jnp.where(ids == skel[j], 1.0, 0.0)
    red_t = jnp.where(ids == red[j], 1.0, 0.0)
    order = jnp.where(ids[:size] == pivot[j], 1.0, 0.0).astype(BF16)
    spread = dot(skel_t.astype(BF16), beside(interp, j))
    q_t = cat(1, red_t, jnp.zeros_like(red_t)) - spread
    par[j, 0 : 2 * size, :] = q_t.T.astype(BF16)
    turned = dot_nt(above(inverse, j), order).astype(BF16)
    par[j, 2 * size : 3 * size, :] = paired(turned)
    pick[j] = cat(1, skel_t, red_t).T[:size].astype(BF16)


def read_params(block):
    size = block.shape[0] // 3
    q_re, q_im, inv = block[:size], block[size : 2 * size], block[2 * size :]
    real_row, imag_row = cat(1, q_re, -q_im), cat(1, q_im, q_re)
    q_mix = cat(0, real_row, imag_row)
    e_mix = cat(0, real_row, -imag_row, imag_row, real_row)
    inv_re, inv_im = inv[:, :size], inv[:, size:]
    inv_mix = cat(0, cat(1, inv_re, -inv_im), cat(1, inv_im, inv_re))
    return q_mix, e_mix, inv_mix


def factors(params, right_op):
    q_mix, _, inv_mix = params
    return dot(inv_mix, dot(q_mix, right_op).astype(BF16)).astype(BF16)


def kernel(
    self_hbm, coup_hbm, skel_hbm, red_hbm, interp_hbm, pivot_hbm, inverse_hbm,
    factor_out, updated_out, coarse_out,
    own, coup, skel, red, interp, pivot, inverse,
    pick, par, par_x, par_y, extra, extra_y, fac, acc, w_send_x, w_send_y, w_x, w_y,
    self_term, k_own, keep_k, g_own, g_other, updated, coarse,
    in_sem, send_sem, recv_sem, out_sem,
):
    n, points = own.shape[0], own.shape[2]
    half, size = n // 2, skel.shape[2]
    gx, gy = lax.axis_index("gx"), lax.axis_index("gy")
    nx, ny = lax.axis_size("gx"), lax.axis_size("gy")
    x_next, x_back = {"gx": lax.rem(gx + 1, nx)}, {"gx": lax.rem(gx + nx - 1, nx)}
    y_next, y_back = {"gy": lax.rem(gy + 1, ny)}, {"gy": lax.rem(gy + ny - 1, ny)}
    odd = lax.rem(gy, 2)
    partner = {"gy": gy + 1 - 2 * odd}

    barrier = pltpu.get_barrier_semaphore()
    for device in (x_next, x_back, y_next, y_back):
        pl.semaphore_signal(barrier, inc=1, device_id=device, device_id_type=MESH)

    def load(source, target, at):
        copy = pltpu.make_async_copy(source, target, in_sem.at[at])
        copy.start()
        return copy

    small = [
        load(skel_hbm, skel, 0),
        load(red_hbm, red, 1),
        load(interp_hbm.at[:, 0], interp, 2),
        load(pivot_hbm, pivot, 3),
        load(inverse_hbm.at[:, 0], inverse, 4),
    ]
    large = []
    for j in range(n):
        large.append(
            (
                load(coup_hbm.at[j, 0], coup.at[j], 5 + 2 * j),
                load(self_hbm.at[j, 0], own.at[j], 6 + 2 * j),
            )
        )

    def remote(source, target, at, device):
        return pltpu.make_async_remote_copy(
            src_ref=source, dst_ref=target, send_sem=send_sem.at[at],
            recv_sem=recv_sem.at[at], device_id=device, device_id_type=MESH,
        )

    outs = []

    def store(source, target):
        copy = pltpu.make_async_copy(source, target, out_sem.at[len(outs)])
        copy.start()
        outs.append(copy)

    send_par_x = remote(par.at[0], par_x, 0, x_back)
    send_par_y = remote(par, par_y, 1, y_back)
    send_extra = remote(extra, extra_y, 2, y_back)
    send_w_x = remote(w_send_x, w_x, 3, x_next)
    send_k = remote(k_own.at[pl.ds((1 - odd) * half, half)], keep_k, 4, partner)
    send_g = remote(g_own.at[pl.ds((1 - odd) * half, half)], g_other, 5, partner)
    send_fac_x = remote(fac.at[n - 1, 1], factor_out.at[0, 0, 1], 6, x_next)
    send_w_y = [remote(w_send_y.at[j], w_y.at[j], 7 + 2 * j, y_next) for j in range(n)]
    send_fac_y = [
        remote(fac.at[j, 3], factor_out.at[j, 0, 3], 8 + 2 * j, y_next) for j in range(n)
    ]

    def put_factor(j, k, value):
        fac[j, k] = value.reshape(2, size, points)

    for copy in small:
        copy.wait()
    for j in range(n):
        make_params(par, pick, skel, red, interp, pivot, inverse, j)
    pl.semaphore_wait(barrier, 4)
    send_par_y.start()
    send_par_x.start()

    for pair in large:
        for copy in pair:
            copy.wait()
    params = [read_params(par[j]) for j in range(n)]
    made = [
        factors(params[j], cat(1, above(coup, j, 2), above(coup, j, 0), above(own, j)))
        for j in range(n)
    ]
    ends = [
        dot_nt(cat(0, beside(coup, j, 3), beside(coup, j, 1)), params[j][1]).astype(BF16)
        for j in range(n)
    ]
    f_up, f_right, f_own = (
        [made[j][:, k * points : (k + 1) * points] for j in range(n)] for k in range(3)
    )
    w_up = [dot(folded(ends[j][:points]), f_up[j]) for j in range(n)]
    w_right = [dot(folded(ends[j][points:]), f_right[j]) for j in range(n)]
    for j in range(n):
        w_send_y[j] = w_up[j].astype(BF16)
    w_send_x[...] = w_right[n - 1].astype(BF16)
    for copy in send_w_y:
        copy.start()
    send_w_x.start()

    def from_next(next_params, j, k):
        made = factors(next_params, above(coup, j, k))
        put_factor(j, k, made)
        ends = dot_nt(beside(coup, j, k - 1), next_params[1]).astype(BF16)
        return dot(folded(ends), made)

    for j in range(n):
        put_factor(j, 4, f_up[j])
        put_factor(j, 2, f_right[j])
        put_factor(j, 0, f_own[j])
        own_rows = dot(pick[j], beside(own, j)).astype(BF16)
        e_mix = folded(dot_nt(own_rows, params[j][1]).astype(BF16))
        self_term[j] = dot(e_mix, cat(1, f_own[j], f_up[j]))
        extra[j, :size, :] = cat(1, e_mix[:size, :size], e_mix[size:, :size])
        extra[j, size:, :] = pick[j]
        block = above(own, j).astype(F32)
        if j > 0:
            block = block - w_right[j - 1]
        if j < n - 1:
            block = block - from_next(params[j + 1], j, 1)
        acc[j] = block

    send_extra.start()

    for j in range(n):
        for k in (0, 2, 4):
            store(fac.at[j, k], factor_out.at[j, 0, k])
    for j in range(n - 1):
        store(fac.at[j, 1], factor_out.at[j + 1, 0, 1])

    send_par_y.wait_recv()
    send_par_x.wait_recv()
    y_params = [read_params(par_y[j]) for j in range(n)]
    gained = [from_next(y_params[j], j, 3) for j in range(n)]
    gained[n - 1] = gained[n - 1] + from_next(read_params(par_x[...]), n - 1, 1)
    for j in range(n):
        acc[j] = acc[j] - gained[j]
    for copy in send_fac_y:
        copy.start()
    send_fac_x.start()

    send_extra.wait_recv()
    send_w_x.wait_recv()
    for copy in send_w_y:
        copy.wait_recv()

    for j in range(n):
        lower_pick, upper_pick = pick[j], extra_y[j, size:, :]
        rows = folded(dot(lower_pick, beside(coup, j, 2))) - self_term[j, :, points:]
        k_own[j, 0] = paired(dot_nt(rows.astype(BF16), upper_pick).astype(BF16))
        end = extra_y[j, :size, :]
        e_re, e_im = end[:, :size], end[:, size:]
        e_mix = cat(0, cat(1, e_re, -e_im), cat(1, e_im, e_re))
        rows = folded(dot(upper_pick, beside(coup, j, 3))) - dot(e_mix, above(fac, j, 3))
        k_own[j, 1] = paired(dot_nt(rows.astype(BF16), lower_pick).astype(BF16))

    for j in range(n):
        total = acc[j] - w_y[j].astype(F32)
        if j == 0:
            total = total - w_x[...].astype(F32)
        rounded = total.astype(BF16)
        rest = (total - rounded.astype(F32)).astype(BF16)
        updated[j] = rounded.reshape(2, points, points)
        rows = dot(pick[j], cat(1, paired(rounded), paired(rest)))
        rows = rows[:, : 2 * points] + rows[:, 2 * points :]
        rows = (folded(rows) - self_term[j, :, :points]).astype(BF16)
        g_own[j] = paired(dot_nt(rows, pick[j]).astype(BF16))
    send_g.start()
    send_k.start()
    for j in range(n):
        store(updated.at[j], updated_out.at[j, 0])

    send_k.wait_recv()
    send_g.wait_recv()
    for t in range(half):
        mine, other = g_own[odd * half + t], g_other[t]
        lower = jnp.where(odd == 0, mine, other)
        upper = jnp.where(odd == 0, other, mine)
        k_lower, k_upper = (jnp.where(odd == 0, k_own[t, k], keep_k[t, k]) for k in range(2))
        for c in range(2):
            part = slice(c * size, (c + 1) * size)
            coarse[t, c, :size, :] = cat(1, lower[:, part], k_lower[:, part])
            coarse[t, c, size:, :] = cat(1, k_upper[:, part], upper[:, part])
    store(coarse, coarse_out.at[:, 0])

    send_fac_x.wait_recv()
    for copy in send_fac_y:
        copy.wait_recv()
    for copy in [send_par_x, send_par_y, send_w_x, send_extra, send_k, send_g, send_fac_x, *send_w_y, *send_fac_y]:
        copy.wait_send()

    for copy in outs:
        copy.wait()


def hand_over(*refs):
    sources, targets, sem = refs[:3], refs[3:6], refs[6]
    copies = [
        pltpu.make_async_copy(source, target, sem.at[at])
        for at, (source, target) in enumerate(zip(sources, targets))
    ]
    for copy in copies:
        copy.start()
    for copy in copies:
        copy.wait()


def local(self_block, coupling, skeleton, redundant, interp, pivot, pivot_inverse):
    n, _, _, points, _ = self_block.shape
    size, half = skeleton.shape[2], n // 2
    vmem = pltpu.VMEM
    shapes = (
        jax.ShapeDtypeStruct((n, 1, 5, 2, size, points), BF16),
        jax.ShapeDtypeStruct((n, 1, 2, points, points), BF16),
        jax.ShapeDtypeStruct((half, 1, 2, points, points), BF16),
    )
    made = pl.pallas_call(
        kernel,
        out_shape=tuple(pltpu.VMEM(shape.shape, shape.dtype) for shape in shapes),
        in_specs=[pl.BlockSpec(memory_space=pl.ANY)] * 7,
        out_specs=(pl.BlockSpec(memory_space=pl.ANY),) * 3,
        scratch_shapes=[
            vmem((n, 2, points, points), BF16),
            vmem((n, 4, 2, points, points), BF16),
            vmem((n, 1, size), jnp.int32),
            vmem((n, 1, size), jnp.int32),
            vmem((n, 2, size, size), BF16),
            vmem((n, 1, size), jnp.int32),
            vmem((n, 2, size, size), BF16),
            vmem((n, size, points), BF16),
            vmem((n, 3 * size, points), BF16),
            vmem((3 * size, points), BF16),
            vmem((n, 3 * size, points), BF16),
            vmem((n, 2 * size, points), BF16),
            vmem((n, 2 * size, points), BF16),
            vmem((n, 5, 2, size, points), BF16),
            vmem((n, 2 * points, points), F32),
            vmem((2 * points, points), BF16),
            vmem((n, 2 * points, points), BF16),
            vmem((2 * points, points), BF16),
            vmem((n, 2 * points, points), BF16),
            vmem((n, 2 * size, 2 * points), F32),
            vmem((n, 2, size, 2 * size), BF16),
            vmem((half, 2, size, 2 * size), BF16),
            vmem((n, size, 2 * size), BF16),
            vmem((half, size, 2 * size), BF16),
            vmem((n, 2, points, points), BF16),
            vmem((half, 2, points, points), BF16),
            pltpu.SemaphoreType.DMA((5 + 2 * n,)),
            pltpu.SemaphoreType.DMA((7 + 2 * n,)),
            pltpu.SemaphoreType.DMA((7 + 2 * n,)),
            pltpu.SemaphoreType.DMA((5 * n,)),
        ],
        compiler_params=pltpu.CompilerParams(
            collective_id=0, has_side_effects=True, vmem_limit_bytes=62 * 2**20
        ),
    )(self_block, coupling, skeleton, redundant, interp, pivot, pivot_inverse)
    return pl.pallas_call(
        hand_over,
        out_shape=shapes,
        in_specs=[pl.BlockSpec(memory_space=pl.ANY)] * 3,
        out_specs=(pl.BlockSpec(memory_space=pltpu.HBM),) * 3,
        scratch_shapes=[pltpu.SemaphoreType.DMA((3,))],
        compiler_params=pltpu.CompilerParams(vmem_limit_bytes=2**20),
    )(*made)


def solution(mesh):
    box = P("gx", "gy", None, None, None)
    wide = P("gx", "gy", None, None, None, None)
    index = P("gx", "gy", None)
    return jax.shard_map(
        local,
        mesh=mesh,
        in_specs=(box, wide, index, index, box, index, box),
        out_specs=(wide, box, box),
        check_vma=False,
    )
```
